32 devices in a mesh: section: 4 (over x, core), expert: 8 (over z, y).
Axes of the slice: x: 2, y: 2, z: 4, core: 2. Of those that a mesh axis runs over, the one named last changes fastest.
Arguments:
- tokens: bfloat16 [8, 576, 2048], P(None, 'expert'), may hold values from -6 to 6
- w_in: bfloat16 [4, 2048, 2048], P('section', 'expert'), may hold values from -0.125 to 0.125
- w_out: bfloat16 [4, 2048, 2048], P('section', 'expert'), may hold values from -0.125 to 0.125
- router: bfloat16 [2048, 8], replicated, may hold values from -0.125 to 0.125
- exp_in: bfloat16 [8, 2048, 2048], P('expert', None, 'section'), may hold values from -0.125 to 0.125
- exp_out: bfloat16 [8, 2048, 2048], P('expert', 'section'), may hold values from -0.375 to 0.375
- active_rows: int32 [1152], P('expert'), may hold values from 0 to 575, as said below
- active_expert: int32 [1152, 1], P('expert'), may hold values from 0 to 7; in each aligned block of 144 rows (0 to 143, 144 to 287, ...) at most 54 rows name the same one
Outputs:
- updated: bfloat16 [8, 576, 2048], P(None, 'expert', 'section')
The draws below stay inside these ranges and needn't reach their ends.
Inputs may be any that keep to these rules, and one draw needn't show every extreme that they name: `active_rows`: the 144 entries of one token block name distinct rows of its 576 rows. `active_expert`: among the 144 entries of one token block no expert is named more than 54 times.
All inputs are finite; a program needn't handle non-finite values.
Results may differ from the reference program's by a relative error of at most 0.024.
Values may be sent and summed in bfloat16 or wider, within the bound.
A program may use at most 64 MiB of HBM per device.

```python
import math
import jax
import jax.numpy as jnp
import numpy as np
from jax import lax

D = 2048
HID = 2048
EXP_HID = 2048
MB = 8
TOK_DEV = 72
LAYERS = 4
EXPERTS = 8
TOKENS = 576
ROWS_DEV = 576
ACT_DEV = 144
ACTIVE = 1152
CAP = 54
N_EXPERT = 8


def force_member(listing, value):
    present = jnp.any(listing == value)
    return jnp.where(present, listing, listing.at[0].set(value))


def draw_active_rows(key, part):
    keys = jax.random.split(jax.random.fold_in(key, 11), N_EXPERT)

    def one_block(block_key):
        return jax.random.permutation(block_key, ROWS_DEV)[:ACT_DEV].astype(jnp.int32)
    lists = jax.vmap(one_block)(keys)
    lists = lists.at[0].set(force_member(lists[0], ROWS_DEV - 1))
    lists = lists.at[N_EXPERT - 1].set(force_member(lists[N_EXPERT - 1], 0))
    return lists.reshape(ACTIVE).astype(jnp.int32)


def raised(drawn, own_key, source, target, blocks, factor):
    def block_of(dim):
        return (jnp.arange(drawn.shape[dim]) // (drawn.shape[dim] // blocks)).reshape((-1,) + (1,) * (drawn.ndim - 1 - dim))

    first = jax.random.permutation(own_key, blocks)[block_of(target)]
    far = (block_of(target) + blocks // 2) % blocks
    return jnp.where((block_of(source) == first) | (block_of(source) == far), factor * drawn, drawn)


def steps_of(key, shape, pieces, least, top_value):
    level = 1.0
    for dim, blocks in pieces:
        draws = jax.random.uniform(jax.random.fold_in(jax.random.fold_in(key, 6), dim), (blocks,), jnp.float32, least / len(pieces), top_value / len(pieces))
        level = level * jnp.repeat(jnp.exp(draws), shape[dim] // blocks).reshape((-1,) + (1,) * (len(shape) - 1 - dim))
    return level


def shared_out(rng, own, number, rows, count, top, limit, skew):
    sequence = jax.random.permutation(rng, count)
    heavy_load, ordinary = load_shares(count, rows * top, limit, skew, True), load_shares(count, rows * top, limit, skew, False)
    places = jnp.arange(count)

    def named(tallies, offset_by):
        used = int((tallies > 0).sum())
        fixed = max(1, used // 4)
        shifted = fixed + (places - fixed + offset_by * (used - fixed)) % max(1, count - fixed)
        return jnp.zeros((count,), jnp.int32).at[sequence[jnp.where(places < fixed, places, shifted)]].set(jnp.asarray(tallies, jnp.int32))

    tallies = jnp.where(number % 4 == 0, named(heavy_load, number // 4), named(ordinary, number - number // 4 - 1))
    mixed = jax.random.permutation(jax.random.fold_in(own, 3), count)
    source_of, receiver = mixed[0:count // 2 * 2:2], mixed[1:count // 2 * 2:2]
    room = jnp.minimum(tallies[source_of] - 1, limit - tallies[receiver]) // 2
    room = jnp.where((source_of == sequence[0]) | (receiver == sequence[0]) | (tallies[receiver] == 0), 0, jnp.maximum(room, 0))
    shifted = jax.random.randint(jax.random.fold_in(own, 4), (count // 2,), 0, 1 << 20) % (room + 1)
    tallies = tallies.at[source_of].add(-shifted).at[receiver].add(shifted)
    items = jnp.searchsorted(jnp.cumsum(tallies), jnp.arange(rows * top), side="right").astype(jnp.int32)
    grid = items.reshape(top, rows).T
    grid = grid[jax.random.permutation(jax.random.fold_in(own, 1), rows)]
    offset_by = jax.random.randint(jax.random.fold_in(own, 2), (rows, 1), 0, top)
    return jnp.take_along_axis(grid, (jnp.arange(top)[None, :] + offset_by) % top, axis=1)


def load_shares(amount, total, most, lean, full):
    loads = [(1 << 20) // math.isqrt(rank ** lean) + 1 for rank in range(1, amount + 1)]
    largest = most if full else min(most, max(-(-total // amount), total * loads[0] // sum(loads)))
    least = 1 if total - largest >= amount - 1 else 0
    holding, surplus = [largest] + [least] * (amount - 1), total - largest - least * (amount - 1)
    while surplus > 0:
        candidates = [i for i in range(1, amount) if holding[i] < largest] or [i for i in range(1, amount) if holding[i] < most]
        mass, left = sum([loads[i] for i in candidates]), surplus
        for i in candidates:
            extra = min(most - holding[i], max(1, left * loads[i] // mass), surplus)
            holding[i] = holding[i] + extra
            surplus = surplus - extra
    return np.array(holding)


def normal_values(rng, dims, scale, reach, cuts=(), held_as=jnp.bfloat16):
    loudness = steps_of(rng, dims, cuts, -0.22, 0.18) if cuts else 1.0
    result = jax.random.normal(rng, dims, jnp.float32) * scale * loudness
    return jnp.minimum(jnp.maximum(result, -reach), reach).astype(held_as)


def heavy_noise(rng, dims, scale, bound, cuts, heavy, kind=jnp.bfloat16):
    values = scale * jax.random.normal(rng, dims, jnp.float32)
    if cuts:
        values = values * steps_of(rng, dims, cuts, -0.22, 0.18)
    return jnp.clip(raised(values, jax.random.fold_in(rng, 3), *heavy), -bound, bound).astype(kind)


def setup_inputs(seed: int = 0) -> dict:
    key_list = jax.random.split(jax.random.key(seed), 9)
    tokens = normal_values(key_list[0], (MB, TOKENS, D), 1.0, 6.0, ((1, 8),))
    w_in = normal_values(key_list[1], (LAYERS, D, HID), D ** -0.5, 0.125, ((0, 4), (1, 8)))
    w_out = normal_values(key_list[2], (LAYERS, HID, D), HID ** -0.5, 0.125, ((0, 4), (1, 8)))
    router = normal_values(key_list[3], (D, EXPERTS), D ** -0.5, 0.125)
    exp_in = normal_values(key_list[4], (EXPERTS, D, EXP_HID), D ** -0.5, 0.125, ((0, 8), (2, 4)))
    exp_out = heavy_noise(key_list[5], (EXPERTS, EXP_HID, D), (EXP_HID // 4) ** -0.5, 0.375, ((0, 8), (1, 4)), (1, 2, 4, 2.0))
    active_rows = draw_active_rows(jax.random.fold_in(key_list[8], 71), 0)
    active_expert_keys = jax.random.split(jax.random.fold_in(key_list[7], 1), ACTIVE // ACT_DEV)
    active_expert_turns = jax.random.permutation(jax.random.fold_in(key_list[7], 3), ACTIVE // ACT_DEV)
    active_expert = jax.vmap(lambda own, number: shared_out(jax.random.fold_in(key_list[7], 2), own, number, ACT_DEV, EXPERTS, 1, CAP, 2))(active_expert_keys, active_expert_turns).reshape((ACTIVE, 1))
    return {"tokens": tokens, "w_in": w_in, "w_out": w_out, "router": router, "exp_in": exp_in, "exp_out": exp_out, "active_rows": active_rows, "active_expert": active_expert}


def normalize(rows):
    wide = rows.astype(jnp.float32)
    scale = lax.rsqrt(lax.optimization_barrier(jnp.mean(wide * wide, axis=-1, keepdims=True)) + 1e-05)
    return wide * scale

def processor(stream, w_first, w_second):
    normed = normalize(stream).astype(jnp.bfloat16)
    hidden = jax.nn.silu(jnp.dot(normed, w_first, preferred_element_type=jnp.float32)).astype(jnp.bfloat16)
    branch = jnp.dot(hidden, w_second, preferred_element_type=jnp.float32)
    return (stream.astype(jnp.float32) + branch).astype(jnp.bfloat16)

def reference(tokens, w_in, w_out, router, exp_in, exp_out, active_rows, active_expert):
    stream = tokens.reshape(MB * TOKENS, D)
    for layer in range(LAYERS):
        stream = processor(stream, w_in[layer], w_out[layer])
    blocks = stream.reshape(MB, N_EXPERT, TOK_DEV, D).transpose(1, 0, 2, 3).reshape(N_EXPERT, ROWS_DEV, D)
    lists = active_rows.reshape(N_EXPERT, ACT_DEV).astype(jnp.int32)
    chosen = active_expert.reshape(N_EXPERT, ACT_DEV).astype(jnp.int32)
    picked = jnp.take_along_axis(blocks, lists[:, :, None], axis=1)
    contact = normalize(picked).astype(jnp.bfloat16)
    logits = jnp.einsum('nad,de->nae', contact.astype(jnp.float32), router.astype(jnp.float32))
    gate = jax.nn.sigmoid(jnp.take_along_axis(logits, chosen[:, :, None], axis=2)[:, :, 0])
    counts = (chosen[:, :, None] == jnp.arange(EXPERTS, dtype=jnp.int32)[None, None, :]).astype(jnp.int32)
    earlier = jnp.cumsum(counts, axis=1) - counts
    rank = lax.optimization_barrier(jnp.sum(earlier * counts, axis=2))
    position = (chosen * CAP + rank).astype(jnp.int32)
    owners = jnp.arange(N_EXPERT, dtype=jnp.int32)[:, None]
    buffer = jnp.zeros((N_EXPERT, EXPERTS * CAP, D), jnp.bfloat16).at[owners, position].set(contact)
    buffer = buffer.reshape(N_EXPERT, EXPERTS, CAP, D).transpose(1, 0, 2, 3).reshape(EXPERTS, N_EXPERT * CAP, D)

    def run_expert(packed):
        rows, first, second = packed
        hidden = jax.nn.silu(jnp.dot(rows, first, preferred_element_type=jnp.float32)).astype(jnp.bfloat16)
        return jnp.dot(hidden, second, preferred_element_type=jnp.float32)
    values = lax.map(run_expert, (buffer, exp_in, exp_out))
    values = values.reshape(EXPERTS, N_EXPERT, CAP, D).transpose(1, 0, 2, 3).reshape(N_EXPERT, EXPERTS * CAP, D)
    mine = jnp.take_along_axis(values, position[:, :, None], axis=1)
    mixed = blocks.astype(jnp.float32).at[owners, lists].add(gate[:, :, None] * mine)
    mixed = mixed.astype(jnp.bfloat16).reshape(N_EXPERT, MB, TOK_DEV, D).transpose(1, 0, 2, 3)
    return mixed.reshape(MB, TOKENS, D)
```

```python
import functools

import jax
import jax.numpy as jnp
from jax import lax
from jax.experimental import pallas as pl
from jax.experimental.pallas import tpu as pltpu
from jax.sharding import PartitionSpec as P

MESH = pl.DeviceIdType.MESH


def gather_kernel(n_z, n_y, first_ref, second_ref, first_out, second_out, local_sem, send_sem, recv_sem):
    me = lax.axis_index("expert")
    z, y = lax.div(me, n_y), lax.rem(me, n_y)
    rows = first_ref.shape[0]
    outs = (first_out, second_out)
    up, down, right, left = range(4)
    steps = (n_y, -n_y, 1, -1)
    there = (z < n_z - 1, z > 0, y < n_y - 1, y > 0)

    barrier = pltpu.get_barrier_semaphore()
    for way in range(4):

        @pl.when(there[way])
        def _(way=way):
            pl.semaphore_signal(barrier, inc=1, device_id={"expert": me + steps[way]}, device_id_type=MESH)

    pl.semaphore_wait(barrier, sum(near.astype(jnp.int32) for near in there))

    def block(which, owner):
        return outs[which].at[pl.ds(pl.multiple_of(owner * rows, rows), rows)]

    def copy(which, owner, way):
        return pltpu.make_async_remote_copy(
            src_ref=block(which, owner),
            dst_ref=block(which, owner),
            send_sem=send_sem.at[way, which, owner],
            recv_sem=recv_sem.at[which, owner],
            device_id={"expert": me + steps[way]},
            device_id_type=MESH,
        )

    def send(which, owner, ways, finish):
        for way in ways:

            @pl.when(there[way])
            def _(way=way):
                sent = copy(which, owner, way)
                if finish:
                    sent.wait_send()
                else:
                    sent.start()

    def visit(finish):
        for far in range(n_z):
            for which in range(2):
                for sign in (-1, 1) if far else (0,):
                    row = z + sign * far

                    @pl.when((row >= 0) & (row < n_z))
                    def _(which=which, row=row, sign=sign):
                        owner = row * n_y + y
                        if sign and not finish:
                            copy(which, owner, down if sign < 0 else up).wait_recv()
                        onward = {0: (up, down), -1: (up,), 1: (down,)}[sign]
                        send(which, owner, onward + (right, left), finish)

        for far in range(1, n_y):
            for row in range(n_z):
                for which in range(2):
                    for sign in (-1, 1):
                        column = y + sign * far

                        @pl.when((column >= 0) & (column < n_y))
                        def _(which=which, row=row, column=column, sign=sign):
                            owner = row * n_y + column
                            if not finish:
                                copy(which, owner, left if sign < 0 else right).wait_recv()
                            if n_y > 2:
                                send(which, owner, (right,) if sign < 0 else (left,), finish)

    own = [
        pltpu.make_async_copy(ref, block(which, me), local_sem.at[which])
        for which, ref in enumerate((first_ref, second_ref))
    ]
    for each in own:
        each.start()
    for each in own:
        each.wait()
    visit(False)
    visit(True)


def gather_weights(w_first, w_second, n_z, n_y):
    rows, width = w_first.shape
    whole = jax.ShapeDtypeStruct((n_z * n_y * rows, width), w_first.dtype)
    return pl.pallas_call(
        functools.partial(gather_kernel, n_z, n_y),
        out_shape=(whole, whole),
        in_specs=[pl.BlockSpec(memory_space=pl.ANY)] * 2,
        out_specs=(pl.BlockSpec(memory_space=pl.ANY), pl.BlockSpec(memory_space=pl.ANY)),
        scratch_shapes=[
            pltpu.SemaphoreType.DMA((2,)),
            pltpu.SemaphoreType.DMA((4, 2, n_z * n_y)),
            pltpu.SemaphoreType.DMA((2, n_z * n_y)),
        ],
        compiler_params=pltpu.CompilerParams(collective_id=0, has_side_effects=True),
    )(w_first, w_second)


def normalize(rows):
    wide = rows.astype(jnp.float32)
    scale = lax.rsqrt(jnp.mean(wide * wide, axis=-1, keepdims=True) + 1e-05)
    return wide * scale


def processor(stream, w_first, w_second):
    normed = normalize(stream).astype(jnp.bfloat16)
    hidden = jax.nn.silu(jnp.dot(normed, w_first, preferred_element_type=jnp.float32)).astype(
        jnp.bfloat16
    )
    branch = jnp.dot(hidden, w_second, preferred_element_type=jnp.float32)
    return (stream.astype(jnp.float32) + branch).astype(jnp.bfloat16)


def local(n_z, n_y, tokens, w_in, w_out, router, exp_in, exp_out, active_rows, active_expert):
    n_section = lax.axis_size("section")
    section = lax.axis_index("section")
    micro, tok_dev, width = tokens.shape
    rows_dev = micro * tok_dev
    part_width = width // n_section
    last = n_section - 1
    w_first, w_second = gather_weights(w_in[0], w_out[0], n_z, n_y)

    stream = tokens.reshape(rows_dev, width)
    for layer in range(n_section):
        stream = lax.cond(
            section == layer,
            lambda held: processor(held, w_first, w_second),
            lambda held: held,
            stream,
        )
        if layer < last:
            passed = lax.ppermute(stream, "section", [(layer, layer + 1)])
            stream = jnp.where(section == layer + 1, passed, stream)

    n_exp = router.shape[1]
    act_dev = active_rows.shape[0]
    capacity = -(-(3 * act_dev // n_exp) // 8) * 8
    chosen = active_expert[:, 0]
    same = chosen[:, None] == chosen[None, :]
    order = jnp.arange(act_dev, dtype=jnp.int32)
    rank = jnp.sum((same & (order[None, :] < order[:, None])).astype(jnp.int32), axis=1)
    position = chosen * capacity + rank
    places = n_exp * capacity
    onehot = chosen[:, None] == jnp.arange(n_exp, dtype=jnp.int32)[None, :]
    placing = jnp.arange(places, dtype=jnp.int32)[:, None] == position[None, :]
    picking = active_rows[:, None] == jnp.arange(rows_dev, dtype=jnp.int32)[None, :]
    placing = placing.astype(jnp.bfloat16)
    unplacing = jnp.dot(
        picking.T.astype(jnp.bfloat16), placing.T, preferred_element_type=jnp.float32
    ).astype(jnp.bfloat16)

    picked = jnp.dot(
        picking.astype(jnp.bfloat16), stream, preferred_element_type=jnp.float32
    ).astype(jnp.bfloat16)
    contact = normalize(picked).astype(jnp.bfloat16)
    both = jnp.concatenate([stream, contact], axis=0)
    mine = both[:, last * part_width :]
    for target in range(last):
        piece = both[:, target * part_width : (target + 1) * part_width]
        passed = lax.ppermute(piece, "section", [(last, target)])
        mine = jnp.where(section == target, passed, mine)
    base, contact = mine[:rows_dev], mine[rows_dev:]

    router_part = lax.dynamic_slice_in_dim(router, section * part_width, part_width, 0)
    logits = jnp.dot(contact, router_part, preferred_element_type=jnp.float32)
    logits = lax.psum(logits, "section")
    gate = jax.nn.sigmoid(jnp.sum(jnp.where(onehot, logits, 0.0), axis=1))
    gate_row = jnp.sum(jnp.where(picking, gate[:, None], 0.0), axis=0)

    outgoing = jnp.dot(placing, contact, preferred_element_type=jnp.float32).astype(jnp.bfloat16)
    outgoing = outgoing.reshape(n_exp, capacity, part_width)
    arrived = lax.all_to_all(outgoing, "expert", split_axis=0, concat_axis=0, tiled=True)
    rows = lax.all_gather(arrived.reshape(places, part_width), "section", axis=1, tiled=True)
    hidden = jax.nn.silu(jnp.dot(rows, exp_in[0], preferred_element_type=jnp.float32)).astype(
        jnp.bfloat16
    )
    partial_value = jnp.dot(hidden, exp_out[0], preferred_element_type=jnp.float32)
    summed = lax.psum_scatter(
        partial_value.astype(jnp.bfloat16), "section", scatter_dimension=1, tiled=True
    )
    returned = lax.all_to_all(
        summed.reshape(n_exp, capacity, part_width), "expert", split_axis=0, concat_axis=0, tiled=True
    ).reshape(places, part_width)
    value = jnp.dot(unplacing, returned, preferred_element_type=jnp.float32)
    mixed = base.astype(jnp.float32) + gate_row[:, None] * value
    return mixed.astype(jnp.bfloat16).reshape(micro, tok_dev, part_width)


def solution(mesh):
    n_y = mesh.shape["section"] // 2
    n_z = mesh.shape["expert"] // n_y
    return jax.shard_map(
        functools.partial(local, n_z, n_y),
        mesh=mesh,
        in_specs=(
            P(None, "expert", None),
            P("section", "expert", None),
            P("section", "expert", None),
            P(),
            P("expert", None, "section"),
            P("expert", "section", None),
            P("expert"),
            P("expert", None),
        ),
        out_specs=P(None, "expert", "section"),
        check_vma=False,
    )
```

```python
import functools

import jax
import jax.numpy as jnp
from jax import lax
from jax.experimental import pallas as pl
from jax.experimental.pallas import tpu as pltpu
from jax.sharding import PartitionSpec as P

MESH = pl.DeviceIdType.MESH


def gather_kernel(n_z, n_y, first_ref, second_ref, first_out, second_out, local_sem, send_sem, recv_sem):
    me = lax.axis_index("expert")
    z, y = lax.div(me, n_y), lax.rem(me, n_y)
    rows = first_ref.shape[0]
    outs = (first_out, second_out)
    up, down, right, left = range(4)
    steps = (n_y, -n_y, 1, -1)
    there = (z < n_z - 1, z > 0, y < n_y - 1, y > 0)

    barrier = pltpu.get_barrier_semaphore()
    for way in range(4):

        @pl.when(there[way])
        def _(way=way):
            pl.semaphore_signal(barrier, inc=1, device_id={"expert": me + steps[way]}, device_id_type=MESH)

    pl.semaphore_wait(barrier, sum(near.astype(jnp.int32) for near in there))

    def block(which, owner):
        return outs[which].at[pl.ds(pl.multiple_of(owner * rows, rows), rows)]

    def copy(which, owner, way):
        return pltpu.make_async_remote_copy(
            src_ref=block(which, owner),
            dst_ref=block(which, owner),
            send_sem=send_sem.at[way, which, owner],
            recv_sem=recv_sem.at[which, owner],
            device_id={"expert": me + steps[way]},
            device_id_type=MESH,
        )

    def send(which, owner, ways, finish):
        for way in ways:

            @pl.when(there[way])
            def _(way=way):
                sent = copy(which, owner, way)
                if finish:
                    sent.wait_send()
                else:
                    sent.start()

    def visit(finish):
        for far in range(n_z):
            for which in range(2):
                for sign in (-1, 1) if far else (0,):
                    row = z + sign * far

                    @pl.when((row >= 0) & (row < n_z))
                    def _(which=which, row=row, sign=sign):
                        owner = row * n_y + y
                        if sign and not finish:
                            copy(which, owner, down if sign < 0 else up).wait_recv()
                        onward = {0: (up, down), -1: (up,), 1: (down,)}[sign]
                        send(which, owner, onward + (right, left), finish)

        for far in range(1, n_y):
            for row in range(n_z):
                for which in range(2):
                    for sign in (-1, 1):
                        column = y + sign * far

                        @pl.when((column >= 0) & (column < n_y))
                        def _(which=which, row=row, column=column, sign=sign):
                            owner = row * n_y + column
                            if not finish:
                                copy(which, owner, left if sign < 0 else right).wait_recv()
                            if n_y > 2:
                                send(which, owner, (right,) if sign < 0 else (left,), finish)

    own = [
        pltpu.make_async_copy(ref, block(which, me), local_sem.at[which])
        for which, ref in enumerate((first_ref, second_ref))
    ]
    for each in own:
        each.start()
    for each in own:
        each.wait()
    visit(False)
    visit(True)


def gather_weights(w_first, w_second, n_z, n_y):
    rows, width = w_first.shape
    whole = jax.ShapeDtypeStruct((n_z * n_y * rows, width), w_first.dtype)
    return pl.pallas_call(
        functools.partial(gather_kernel, n_z, n_y),
        out_shape=(whole, whole),
        in_specs=[pl.BlockSpec(memory_space=pl.ANY)] * 2,
        out_specs=(pl.BlockSpec(memory_space=pl.ANY), pl.BlockSpec(memory_space=pl.ANY)),
        scratch_shapes=[
            pltpu.SemaphoreType.DMA((2,)),
            pltpu.SemaphoreType.DMA((4, 2, n_z * n_y)),
            pltpu.SemaphoreType.DMA((2, n_z * n_y)),
        ],
        compiler_params=pltpu.CompilerParams(collective_id=0, has_side_effects=True),
    )(w_first, w_second)


def normalize(rows):
    wide = rows.astype(jnp.float32)
    scale = lax.rsqrt(jnp.mean(wide * wide, axis=-1, keepdims=True) + 1e-05)
    return wide * scale


def processor(stream, w_first, w_second):
    normed = normalize(stream).astype(jnp.bfloat16)
    hidden = jax.nn.silu(jnp.dot(normed, w_first, preferred_element_type=jnp.float32)).astype(
        jnp.bfloat16
    )
    branch = jnp.dot(hidden, w_second, preferred_element_type=jnp.float32)
    return (stream.astype(jnp.float32) + branch).astype(jnp.bfloat16)


def local(n_z, n_y, tokens, w_in, w_out, router, exp_in, exp_out, active_rows, active_expert):
    n_section = lax.axis_size("section")
    section = lax.axis_index("section")
    micro, tok_dev, width = tokens.shape
    rows_dev = micro * tok_dev
    part_width = width // n_section
    last = n_section - 1
    w_first, w_second = gather_weights(w_in[0], w_out[0], n_z, n_y)

    chunks = 2
    streams = list(tokens.reshape(chunks, rows_dev // chunks, width))
    for tick in range(chunks + last):
        for index in range(chunks):
            layer = tick - index
            if not 0 <= layer <= last:
                continue
            stream = lax.cond(
                section == layer,
                lambda held: processor(held, w_first, w_second),
                lambda held: held,
                streams[index],
            )
            if layer < last:
                passed = lax.ppermute(stream, "section", [(layer, layer + 1)])
                stream = jnp.where(section == layer + 1, passed, stream)
            streams[index] = stream
    stream = jnp.concatenate(streams, axis=0)

    n_exp = router.shape[1]
    act_dev = active_rows.shape[0]
    capacity = -(-(3 * act_dev // n_exp) // 8) * 8
    chosen = active_expert[:, 0]
    same = chosen[:, None] == chosen[None, :]
    order = jnp.arange(act_dev, dtype=jnp.int32)
    rank = jnp.sum((same & (order[None, :] < order[:, None])).astype(jnp.int32), axis=1)
    position = chosen * capacity + rank
    places = n_exp * capacity
    onehot = chosen[:, None] == jnp.arange(n_exp, dtype=jnp.int32)[None, :]
    placing = jnp.arange(places, dtype=jnp.int32)[:, None] == position[None, :]
    picking = active_rows[:, None] == jnp.arange(rows_dev, dtype=jnp.int32)[None, :]
    placing = placing.astype(jnp.bfloat16)
    unplacing = jnp.dot(
        picking.T.astype(jnp.bfloat16), placing.T, preferred_element_type=jnp.float32
    ).astype(jnp.bfloat16)

    picked = jnp.dot(
        picking.astype(jnp.bfloat16), stream, preferred_element_type=jnp.float32
    ).astype(jnp.bfloat16)
    contact = normalize(picked).astype(jnp.bfloat16)
    both = jnp.concatenate([stream, contact], axis=0)
    mine = both[:, last * part_width :]
    for target in range(last):
        piece = both[:, target * part_width : (target + 1) * part_width]
        passed = lax.ppermute(piece, "section", [(last, target)])
        mine = jnp.where(section == target, passed, mine)
    base, contact = mine[:rows_dev], mine[rows_dev:]

    router_part = lax.dynamic_slice_in_dim(router, section * part_width, part_width, 0)
    logits = jnp.dot(contact, router_part, preferred_element_type=jnp.float32)
    logits = lax.psum(logits, "section")
    gate = jax.nn.sigmoid(jnp.sum(jnp.where(onehot, logits, 0.0), axis=1))
    gate_row = jnp.sum(jnp.where(picking, gate[:, None], 0.0), axis=0)

    outgoing = jnp.dot(placing, contact, preferred_element_type=jnp.float32).astype(jnp.bfloat16)
    outgoing = outgoing.reshape(n_exp, capacity, part_width)
    arrived = lax.all_to_all(outgoing, "expert", split_axis=0, concat_axis=0, tiled=True)
    rows = lax.all_gather(arrived.reshape(places, part_width), "section", axis=1, tiled=True)
    hidden = jax.nn.silu(jnp.dot(rows, exp_in[0], preferred_element_type=jnp.float32)).astype(
        jnp.bfloat16
    )
    partial_value = jnp.dot(hidden, exp_out[0], preferred_element_type=jnp.float32)
    summed = lax.psum_scatter(
        partial_value.astype(jnp.bfloat16), "section", scatter_dimension=1, tiled=True
    )
    returned = lax.all_to_all(
        summed.reshape(n_exp, capacity, part_width), "expert", split_axis=0, concat_axis=0, tiled=True
    ).reshape(places, part_width)
    value = jnp.dot(unplacing, returned, preferred_element_type=jnp.float32)
    mixed = base.astype(jnp.float32) + gate_row[:, None] * value
    return mixed.astype(jnp.bfloat16).reshape(micro, tok_dev, part_width)


def solution(mesh):
    n_y = mesh.shape["section"] // 2
    n_z = mesh.shape["expert"] // n_y
    return jax.shard_map(
        functools.partial(local, n_z, n_y),
        mesh=mesh,
        in_specs=(
            P(None, "expert", None),
            P("section", "expert", None),
            P("section", "expert", None),
            P(),
            P("expert", None, "section"),
            P("expert", "section", None),
            P("expert"),
            P("expert", None),
        ),
        out_specs=P(None, "expert", "section"),
        check_vma=False,
    )
```
